32 devices in a mesh: mic: 16 (over z, y, x), seg: 2 (over core).
Axes of the slice: x: 2, y: 2, z: 4, core: 2. Of those that a mesh axis runs over, the one named last changes fastest.
Arguments:
- pressure: bfloat16 [2, 4, 64, 8192], P(None, None, 'seg', 'mic'), may hold values from -6 to 6
- harmonics: bfloat16 [8192, 4096], P('mic'), may hold values from -0.0625 to 0.0625
- steering: bfloat16 [4096, 2048], P(None, 'mic'), may hold values from -0.09375 to 0.09375
- radial_mag: float32 [4, 64], replicated, may hold values from 0.5 to 2
- radial_phase: float32 [4, 64], replicated, may hold values from -3.140625 to 3.140625
- noise: float32 [4, 4096], replicated, may hold values from 0.5 to 8
Outputs:
- beam_power: float32 [4, 2048], P(None, 'mic')
The draws below stay inside these ranges and needn't reach their ends.
All inputs are finite; a program needn't handle non-finite values.
Results may differ from the reference program's by a relative error of at most 0.00057.
Values may be sent and summed in bfloat16 or wider, within the bound.
A program may use at most 64 MiB of HBM per device.

```python
import math
import jax
import jax.numpy as jnp
from jax import lax

ORDERS = 64
K = 4096
BINS = 4
SEGMENTS = 64
MIC_DEV = 512
MICS = 8192
DIRS = 2048


def level_of(own_key, dims, cuts, low, high):
    level, own = 1.0, jax.random.fold_in(own_key, 6)
    for position, shards_of in cuts:
        heights = jnp.exp(jax.random.uniform(jax.random.fold_in(own, position), (shards_of,), jnp.float32, low / len(cuts), high / len(cuts)))
        level = level * jnp.repeat(heights, dims[position] // shards_of).reshape([-1 if axis == position else 1 for axis in range(len(dims))])
    return level


def centred(stream_key, extent, scale, limit, split=(), held_as=jnp.bfloat16):
    entries = jax.random.normal(stream_key, extent, jnp.float32) * scale
    if len(split) > 0:
        entries = level_of(stream_key, extent, split, -0.22, 0.18) * entries
    return jnp.clip(entries, min=-limit, max=limit).astype(held_as)


def setup_inputs(seed: int = 0) -> dict:
    arg_keys = jax.random.split(jax.random.key(seed), 7)
    return {
        "pressure": centred(arg_keys[0], (2, BINS, SEGMENTS, MICS), 1.0, 6.0, ((2, 2), (3, 16))),
        "harmonics": centred(arg_keys[1], (MICS, K), MICS ** -0.5, 0.0625, ((0, 16),)),
        "steering": centred(arg_keys[2], (K, DIRS), K ** -0.5, 0.09375, ((1, 16),)),
        "radial_mag": jnp.clip(jnp.exp(jax.random.uniform(arg_keys[3], (BINS, ORDERS), jnp.float32, math.log(0.5), math.log(2.0))), 0.5, 2.0),
        "radial_phase": jnp.clip(jax.random.uniform(arg_keys[4], (BINS, ORDERS), jnp.float32, -3.140625, 3.140625), -3.140625, 3.140625),
        "noise": jnp.clip(jnp.exp(jax.random.uniform(arg_keys[5], (BINS, K), jnp.float32, math.log(0.5), math.log(8.0))), 0.5, 8.0),
    }


def order_lookup(table, count, start):
    orders = table.shape[1]
    index = start + jnp.arange(count, dtype=jnp.int32)
    squares = (jnp.arange(1, orders, dtype=jnp.int32) ** 2)
    level = jnp.sum((index[:, None] >= squares[None, :]).astype(jnp.int32), axis=1)
    select = level[:, None] == jnp.arange(orders, dtype=jnp.int32)[None, :]
    return jnp.sum(jnp.where(select[:, None, :], table[None, :, :], jnp.float32(0.0)), axis=2)


def reference(pressure, harmonics, steering, radial_mag, radial_phase, noise):
    rows = pressure.reshape(2 * BINS * SEGMENTS, MICS)
    blocks = MICS // MIC_DEV

    def add_block(total, which):
        part = lax.dynamic_slice_in_dim(rows, which * MIC_DEV, MIC_DEV, 1).astype(jnp.float32)
        table = lax.dynamic_slice_in_dim(harmonics, which * MIC_DEV, MIC_DEV, 0).astype(jnp.float32)
        return total + jnp.dot(part, table, precision=lax.Precision.HIGHEST), None

    coeff, _ = lax.scan(add_block, jnp.zeros((2 * BINS * SEGMENTS, K), jnp.float32), jnp.arange(blocks, dtype=jnp.int32))
    coeff = coeff.reshape(2, BINS, SEGMENTS, K)
    power = jnp.sum(coeff[0] * coeff[0] + coeff[1] * coeff[1], axis=1) / SEGMENTS
    mag = order_lookup(radial_mag, K, 0).T
    phi = order_lookup(radial_phase, K, 0).T
    gain = power / (power + noise) / mag
    cosine = jnp.cos(phi)[:, None, :]
    sine = jnp.sin(phi)[:, None, :]
    gain = gain[:, None, :]
    real_part = gain * (coeff[0] * cosine + coeff[1] * sine)
    imag_part = gain * (coeff[1] * cosine - coeff[0] * sine)
    equalized = jnp.stack([real_part, imag_part]).astype(jnp.bfloat16)
    beam = jnp.dot(equalized.reshape(-1, K).astype(jnp.float32), steering.astype(jnp.float32), precision=lax.Precision.HIGHEST)
    beam = beam.reshape(2, BINS, SEGMENTS, DIRS)
    return jnp.sum(beam[0] * beam[0] + beam[1] * beam[1], axis=1) / SEGMENTS
```

```python
import functools

import jax
import jax.numpy as jnp
from jax import lax
from jax.experimental import pallas as pl
from jax.experimental.pallas import tpu as pltpu
from jax.sharding import PartitionSpec as P

MESH = pl.DeviceIdType.MESH
HALF = 128
OFFSET = 2.5


def order_lookup(table, count, start):
    orders = table.shape[1]
    index = start + jnp.arange(count, dtype=jnp.int32)
    squares = jnp.arange(1, orders, dtype=jnp.int32) ** 2
    level = jnp.sum((index[:, None] >= squares[None, :]).astype(jnp.int32), axis=1)
    select = level[:, None] == jnp.arange(orders, dtype=jnp.int32)[None, :]
    return jnp.sum(jnp.where(select[:, None, :], table[None, :, :], jnp.float32(0.0)), axis=2)


def shards(pressure, harmonics, steering, radial_mag, radial_phase, noise):
    bins = pressure.shape[1]
    seg_local = pressure.shape[2]
    rows = 2 * bins * seg_local
    segments = seg_local * lax.axis_size("seg")
    flat = pressure.reshape(rows, pressure.shape[3])
    local_terms = lax.dot_general(
        harmonics, flat, (((0,), (1,)), ((), ())), preferred_element_type=jnp.float32
    )
    owned = lax.psum_scatter(local_terms, "mic", scatter_dimension=0, tiled=True)
    count = owned.shape[0]
    first = lax.axis_index("mic") * count
    coeff = owned.reshape(count, 2, bins, seg_local)
    local_power = jnp.sum(coeff[:, 0] * coeff[:, 0] + coeff[:, 1] * coeff[:, 1], axis=2)
    power = lax.psum(local_power, "seg") / segments
    noise_part = lax.dynamic_slice_in_dim(noise, first, count, 1).T
    mag = order_lookup(radial_mag, count, first)
    phi = order_lookup(radial_phase, count, first)
    gain = (power / (power + noise_part) / mag)[:, :, None]
    cosine = jnp.cos(phi)[:, :, None]
    sine = jnp.sin(phi)[:, :, None]
    real_part = gain * (coeff[:, 0] * cosine + coeff[:, 1] * sine)
    imag_part = gain * (coeff[:, 1] * cosine - coeff[:, 0] * sine)
    equalized = jnp.stack([real_part, imag_part], axis=1).astype(jnp.bfloat16).reshape(count, rows)
    equalized = lax.all_gather(equalized, "mic", axis=0, tiled=True)
    beam = lax.dot_general(
        steering, equalized, (((0,), (0,)), ((), ())), preferred_element_type=jnp.float32
    )
    beam = beam.reshape(steering.shape[1], 2, bins, seg_local)
    local_beam = jnp.sum(beam[:, 0] * beam[:, 0] + beam[:, 1] * beam[:, 1], axis=2)
    total = lax.psum(local_beam, "seg") / segments
    return total.T


def encode(value):
    square = value * value
    return (square * (value * jnp.abs(value))).astype(jnp.bfloat16)


def decode(code):
    code = code.astype(jnp.float32)
    size = jnp.abs(code)
    root = lax.rsqrt(lax.rsqrt(jnp.maximum(size, 1e-37)))
    return jnp.where(code < 0, -root, jnp.where(code > 0, root, 0.0))


def schedule(bins, bits):
    length = [2.6] + [2.0] + [1.5] * (bits - 2)
    after = length + [1.5] + length[::-1]
    at, events = 0.0, []
    for step in range(len(after) + 1):
        for b in range(bins):
            events.append((at + OFFSET * b, -step, b))
        if step < len(after):
            at += after[step]
    return [(b, -negative) for _, negative, b in sorted(events)]


def kernel(
    n, bits, seg_local,
    pressure, harmonics, steering, mag, phase, noise, out,
    pbuf, hbuf, sbuf, tables, acc, code_out, code_in, gathered,
    power_out, power_in, beam_out, beam_in,
    local_sem, rs_send, rs_recv, ag_send, ag_recv, pw_send, pw_recv, bm_send, bm_recv,
):
    bins, orders_count = mag.shape
    rows = 2 * seg_local
    segments = seg_local * 2
    me, core = lax.axis_index("mic"), lax.axis_index("seg")
    step_of = [(1 << b) * (1 - 2 * ((me // (1 << b)) % 2)) for b in range(bits)]
    orders = ([0, 1] + list(range(2, bits)), [1, 0] + list(range(2, bits)))

    def owner(r):
        return me + sum(step_of[b] for b in range(bits) if (r >> b) & 1)

    def slot(h, r):
        return sum(((r >> b) & 1) << (bits - 1 - j) for j, b in enumerate(orders[h]))

    def near(bit):
        return (me + step_of[bit], core)

    other = (me, 1 - core)

    sequence = sorted(range(n), key=lambda r: (-(r & 1), -(r & 2), r))
    width = 2 * HALF
    loads = {"p": pltpu.make_async_copy(pressure, pbuf, local_sem.at[0])}
    loads["p"].start()
    for r in sequence:
        first = pl.multiple_of(owner(r) * width, width)
        loads["h", r] = pltpu.make_async_copy(
            harmonics.at[:, pl.ds(first, width)], hbuf.at[r], local_sem.at[1 + r]
        )
        loads["h", r].start()
    barrier = pltpu.get_barrier_semaphore()
    for b in range(bits):
        pl.semaphore_signal(barrier, inc=1, device_id=near(b), device_id_type=MESH)
    pl.semaphore_signal(barrier, inc=1, device_id=other, device_id_type=MESH)
    for r in range(n):
        first = pl.multiple_of(owner(r) * width, width)
        loads["s", r] = pltpu.make_async_copy(
            steering.at[pl.ds(first, width), :], sbuf.at[r], local_sem.at[1 + n + r]
        )
        loads["s", r].start()

    sends = []

    def remote(src, dst, send_sem, recv_sem, device):
        copy = pltpu.make_async_remote_copy(
            src_ref=src, dst_ref=dst, send_sem=send_sem, recv_sem=recv_sem,
            device_id=device, device_id_type=MESH,
        )
        copy.start()
        sends.append(copy)
        return copy

    scatter, gather, powers = {}, {}, {}

    def send_scatter(b, h, j):
        half = 1 << (bits - 1 - j)
        scatter[b, h, j] = remote(
            code_out.at[b, h, pl.ds(half, half)], code_in.at[b, h, pl.ds(half, half)],
            rs_send.at[b, h, j], rs_recv.at[b, h, j], near(orders[h][j]),
        )

    def send_gather(b, h, j):
        half = 1 << (bits - 1 - j)
        gather[b, h, j] = remote(
            gathered.at[b, h, pl.ds(0, half)], gathered.at[b, h, pl.ds(half, half)],
            ag_send.at[b, h, j], ag_recv.at[b, h, j], near(orders[h][j]),
        )

    events = schedule(bins, bits)
    early = 0
    while events[early][1] == 0:
        early += 1

    loads["p"].wait()
    for count, r in enumerate(sequence):
        loads["h", r].wait()
        part = jnp.dot(pbuf[...], hbuf[r], preferred_element_type=jnp.float32)
        for h in range(2):
            where = slot(h, r)
            for b in range(bins):
                for c in range(2):
                    first = (c * bins + b) * seg_local
                    block = part[first:first + seg_local, h * HALF:(h + 1) * HALF]
                    if where >= n // 2:
                        code_out[b, h, where, c * seg_local:(c + 1) * seg_local, :] = encode(block)
                    else:
                        acc[b, h, where, c * seg_local:(c + 1) * seg_local, :] = block
        if count == n // 2 - 1:
            pl.semaphore_wait(barrier, bits + 1)
            for b, _ in events[:early]:
                send_scatter(b, 0, 0)
        if count == 3 * n // 4 - 1:
            for b, _ in events[:early]:
                send_scatter(b, 1, 0)

    index = me * width + lax.broadcasted_iota(jnp.int32, (orders_count, width), 1)
    order = lax.broadcasted_iota(jnp.int32, (orders_count, width), 0)
    last = order == orders_count - 1
    select = (index >= order * order) & ((index < (order + 1) * (order + 1)) | last)
    chosen = jnp.where(select, 1.0, 0.0).astype(jnp.float32)
    for t, table in enumerate((mag[...], jnp.cos(phase[...]), jnp.sin(phase[...]))):
        tables[t] = jnp.dot(
            table, chosen, precision=lax.Precision.HIGHEST, preferred_element_type=jnp.float32
        )
    tables[3] = noise[:, pl.ds(pl.multiple_of(me * width, width), width)]
    for r in range(n):
        loads["s", r].wait()

    def reduce_step(b, j):
        half = 1 << (bits - 1 - j)
        for h in range(2):
            scatter[b, h, j].wait_recv()
            if half == 1:
                coeff = acc[b, h, 0] + decode(code_in[b, h, 1])
                acc[b, h, 0] = coeff
                power_out[b, h] = jnp.sum((coeff * coeff).reshape(rows // 8, 8, HALF), axis=0)
                continue
            low = half // 2
            code_out[b, h, low:half] = encode(
                acc[b, h, low:half] + decode(code_in[b, h, half + low:2 * half])
            )
            send_scatter(b, h, j + 1)
            acc[b, h, 0:low] = acc[b, h, 0:low] + decode(code_in[b, h, half:half + low])
        if half == 1:
            powers[b] = remote(
                power_out.at[b], power_in.at[b], pw_send.at[b], pw_recv.at[b], other
            )

    def equalize_step(b):
        powers[b].wait_recv()
        for h in range(2):
            power = jnp.sum(power_out[b, h] + power_in[b, h], axis=0, keepdims=True) / segments
            lanes = slice(h * HALF, (h + 1) * HALF)
            gain = power / (power + tables[3, b:b + 1, lanes]) / tables[0, b:b + 1, lanes]
            cosine, sine = tables[1, b:b + 1, lanes], tables[2, b:b + 1, lanes]
            real, imag = acc[b, h, 0, 0:seg_local, :], acc[b, h, 0, seg_local:rows, :]
            gathered[b, h, 0, 0:seg_local, :] = (gain * (real * cosine + imag * sine)).astype(jnp.bfloat16)
            gathered[b, h, 0, seg_local:rows, :] = (gain * (imag * cosine - real * sine)).astype(jnp.bfloat16)
            send_gather(b, h, bits - 1)

    def gather_step(b, j):
        for h in range(2):
            gather[b, h, j].wait_recv()
            if j > 0:
                send_gather(b, h, j - 1)
        if j == 0:
            beam = jnp.zeros((rows, out.shape[1]), jnp.float32)
            for r in range(n):
                left = jnp.concatenate([gathered[b, 0, slot(0, r)], gathered[b, 1, slot(1, r)]], axis=1)
                beam = beam + jnp.dot(left, sbuf[r], preferred_element_type=jnp.float32)
            beam_out[b] = jnp.sum((beam * beam).reshape(rows // 8, 8, out.shape[1]), axis=0)

    for b, step in events[early:]:
        if step == 0:
            send_scatter(b, 0, 0)
            send_scatter(b, 1, 0)
        elif step <= bits:
            reduce_step(b, step - 1)
        elif step == bits + 1:
            equalize_step(b)
        else:
            gather_step(b, 2 * bits + 1 - step)

    final = remote(beam_out, beam_in, bm_send.at[0], bm_recv.at[0], other)
    final.wait_recv()
    for b in range(bins):
        out[b:b + 1, :] = jnp.sum(beam_out[b] + beam_in[b], axis=0, keepdims=True) / segments
    for copy in sends:
        copy.wait_send()


def fused(n, bits, pressure, harmonics, steering, radial_mag, radial_phase, noise):
    _, bins, seg_local, mics = pressure.shape
    rows = 2 * seg_local
    dirs = steering.shape[1]
    width = 2 * HALF
    f32, bf16 = jnp.float32, jnp.bfloat16
    dma = pltpu.SemaphoreType.DMA
    anywhere, vmem = pl.BlockSpec(memory_space=pl.ANY), pl.BlockSpec(memory_space=pltpu.VMEM)
    return pl.pallas_call(
        functools.partial(kernel, n, bits, seg_local),
        out_shape=jax.ShapeDtypeStruct((bins, dirs), f32),
        in_specs=[anywhere] * 3 + [vmem] * 3,
        out_specs=vmem,
        scratch_shapes=[
            pltpu.VMEM((rows * bins, mics), bf16),
            pltpu.VMEM((n, mics, width), bf16),
            pltpu.VMEM((n, width, dirs), bf16),
            pltpu.VMEM((4, bins, width), f32),
            pltpu.VMEM((bins, 2, n // 2, rows, HALF), f32),
            pltpu.VMEM((bins, 2, n, rows, HALF), bf16),
            pltpu.VMEM((bins, 2, n, rows, HALF), bf16),
            pltpu.VMEM((bins, 2, n, rows, HALF), bf16),
            pltpu.VMEM((bins, 2, 8, HALF), f32),
            pltpu.VMEM((bins, 2, 8, HALF), f32),
            pltpu.VMEM((bins, 8, dirs), f32),
            pltpu.VMEM((bins, 8, dirs), f32),
            dma((1 + 2 * n,)),
            dma((bins, 2, bits)),
            dma((bins, 2, bits)),
            dma((bins, 2, bits)),
            dma((bins, 2, bits)),
            dma((bins,)),
            dma((bins,)),
            dma((1,)),
            dma((1,)),
        ],
        compiler_params=pltpu.CompilerParams(
            collective_id=0, has_side_effects=True, vmem_limit_bytes=44 * 2**20
        ),
    )(
        pressure.reshape(rows * bins, mics), harmonics, steering,
        radial_mag, radial_phase, noise,
    )


def solution(mesh):
    placed = (P(None, None, "seg", "mic"), P("mic", None), P(None, "mic"), P(), P(), P())
    n = mesh.shape["mic"]
    bits = n.bit_length() - 1

    def run(pressure, harmonics, *rest):
        fits = n == 1 << bits and bits >= 2 and harmonics.shape[1] == 2 * HALF * n
        fits = fits and mesh.shape["seg"] == 2 and pressure.shape[2] % 16 == 0
        if fits:
            return fused(n, bits, pressure, harmonics, *rest)
        return shards(pressure, harmonics, *rest)

    return jax.shard_map(
        run, mesh=mesh, in_specs=placed, out_specs=P(None, "mic"), check_vma=False
    )
```

```python
import functools

import jax
import jax.numpy as jnp
from jax import lax
from jax.experimental import pallas as pl
from jax.experimental.pallas import tpu as pltpu
from jax.sharding import PartitionSpec as P

MESH = pl.DeviceIdType.MESH
HALF = 128
OFFSET = 4.0
AHEAD = 1
LENGTHS = (2.5, 3.5, 2.0, 3.5, 2.5, 4.0, 0.0)


def order_lookup(table, count, start):
    orders = table.shape[1]
    index = start + jnp.arange(count, dtype=jnp.int32)
    squares = jnp.arange(1, orders, dtype=jnp.int32) ** 2
    level = jnp.sum((index[:, None] >= squares[None, :]).astype(jnp.int32), axis=1)
    select = level[:, None] == jnp.arange(orders, dtype=jnp.int32)[None, :]
    return jnp.sum(jnp.where(select[:, None, :], table[None, :, :], jnp.float32(0.0)), axis=2)


def shards(pressure, harmonics, steering, radial_mag, radial_phase, noise):
    bins = pressure.shape[1]
    seg_local = pressure.shape[2]
    rows = 2 * bins * seg_local
    segments = seg_local * lax.axis_size("seg")
    flat = pressure.reshape(rows, pressure.shape[3])
    local_terms = lax.dot_general(
        harmonics, flat, (((0,), (1,)), ((), ())), preferred_element_type=jnp.float32
    )
    owned = lax.psum_scatter(local_terms, "mic", scatter_dimension=0, tiled=True)
    count = owned.shape[0]
    first = lax.axis_index("mic") * count
    coeff = owned.reshape(count, 2, bins, seg_local)
    local_power = jnp.sum(coeff[:, 0] * coeff[:, 0] + coeff[:, 1] * coeff[:, 1], axis=2)
    power = lax.psum(local_power, "seg") / segments
    noise_part = lax.dynamic_slice_in_dim(noise, first, count, 1).T
    mag = order_lookup(radial_mag, count, first)
    phi = order_lookup(radial_phase, count, first)
    gain = (power / (power + noise_part) / mag)[:, :, None]
    cosine = jnp.cos(phi)[:, :, None]
    sine = jnp.sin(phi)[:, :, None]
    real_part = gain * (coeff[:, 0] * cosine + coeff[:, 1] * sine)
    imag_part = gain * (coeff[:, 1] * cosine - coeff[:, 0] * sine)
    equalized = jnp.stack([real_part, imag_part], axis=1).astype(jnp.bfloat16).reshape(count, rows)
    equalized = lax.all_gather(equalized, "mic", axis=0, tiled=True)
    beam = lax.dot_general(
        steering, equalized, (((0,), (0,)), ((), ())), preferred_element_type=jnp.float32
    )
    beam = beam.reshape(steering.shape[1], 2, bins, seg_local)
    local_beam = jnp.sum(beam[:, 0] * beam[:, 0] + beam[:, 1] * beam[:, 1], axis=2)
    total = lax.psum(local_beam, "seg") / segments
    return total.T


def encode(value):
    square = value * value
    return (square * (value * jnp.abs(value))).astype(jnp.bfloat16)


def decode(code):
    code = code.astype(jnp.float32)
    size = jnp.abs(code)
    root = lax.rsqrt(lax.rsqrt(jnp.maximum(size, 1e-37)))
    return jnp.where(code < 0, -root, jnp.where(code > 0, root, 0.0))


def schedule(bins):
    starts = [sum(LENGTHS[:step]) for step in range(len(LENGTHS))]
    events = [(starts[step] + OFFSET * b, -step, b) for step in range(len(LENGTHS)) for b in range(bins)]
    return [(b, 1 - negative) for _, negative, b in sorted(events)]


def kernel(
    n, bits, seg_local,
    pressure, harmonics, steering, mag, phase, noise, out,
    pbuf, hbuf, sbuf, tables, acc, code_out, code_in, gathered,
    power_out, power_in, beam_out, beam_in,
    local_sem, rs_send, rs_recv, ag_send, ag_recv, pw_send, pw_recv, bm_send, bm_recv,
):
    bins, orders_count = mag.shape
    rows = 2 * seg_local
    segments = seg_local * 2
    me, core = lax.axis_index("mic"), lax.axis_index("seg")
    step_of = [(1 << b) * (1 - 2 * ((me // (1 << b)) % 2)) for b in range(bits)]
    rest = n // 4

    def owner(r):
        return me + sum(step_of[b] for b in range(bits) if (r >> b) & 1)

    def slot(h, r):
        x, y = r & 1, (r >> 1) & 1
        return (r >> 2) + rest * ((2 * x + y) if h == 0 else (2 * y + x))

    def near(r):
        return (owner(r), core)

    other = (me, 1 - core)

    sequence = sorted(range(n), key=lambda r: (-(r & 1), -(r & 2), r))
    width = 2 * HALF
    loads = {"p": pltpu.make_async_copy(pressure, pbuf, local_sem.at[0])}
    loads["p"].start()
    for r in sequence:
        first = pl.multiple_of(owner(r) * width, width)
        loads["h", r] = pltpu.make_async_copy(
            harmonics.at[:, pl.ds(first, width)], hbuf.at[r], local_sem.at[1 + r]
        )
        loads["h", r].start()
    barrier = pltpu.get_barrier_semaphore()
    peers = [1, 2] + [4 * q for q in range(1, rest)]
    for r in peers:
        pl.semaphore_signal(barrier, inc=1, device_id=near(r), device_id_type=MESH)
    pl.semaphore_signal(barrier, inc=1, device_id=other, device_id_type=MESH)
    for r in range(n):
        first = pl.multiple_of(owner(r) * width, width)
        loads["s", r] = pltpu.make_async_copy(
            steering.at[pl.ds(first, width), :], sbuf.at[r], local_sem.at[1 + n + r]
        )
        loads["s", r].start()

    sends = []

    def remote(src, dst, send_sem, recv_sem, device):
        copy = pltpu.make_async_remote_copy(
            src_ref=src, dst_ref=dst, send_sem=send_sem, recv_sem=recv_sem,
            device_id=device, device_id_type=MESH,
        )
        copy.start()
        sends.append(copy)
        return copy

    scatter, gather, powers = {}, {}, {}

    def send_scatter(b, h, j):
        half = n >> (j + 1)
        scatter[b, h, j] = remote(
            code_out.at[b, h, pl.ds(half, half)], code_in.at[b, h, pl.ds(half, half)],
            rs_send.at[b, h, j], rs_recv.at[b, h, j], near(1 + (h ^ j)),
        )

    def send_gather(b, h, j):
        half = n >> (j + 1)
        gather[b, h, j] = remote(
            gathered.at[b, h, pl.ds(0, half)], gathered.at[b, h, pl.ds(half, half)],
            ag_send.at[b, h, j], ag_recv.at[b, h, j], near(1 + (h ^ j)),
        )

    def send_rest(b, h, first, target, group, send_sem, recv_sem):
        for q in range(1, rest):
            group[b, h, 1 + q] = remote(
                first(q), target.at[b, h, q],
                send_sem.at[b, h, 1 + q], recv_sem.at[b, h, 1 + q], near(4 * q),
            )

    loads["p"].wait()
    for count, r in enumerate(sequence):
        loads["h", r].wait()
        part = jnp.dot(pbuf[...], hbuf[r], preferred_element_type=jnp.float32)
        for h in range(2):
            where = slot(h, r)
            for b in range(bins):
                for c in range(2):
                    first = (c * bins + b) * seg_local
                    block = part[first:first + seg_local, h * HALF:(h + 1) * HALF]
                    if where >= n // 2:
                        code_out[b, h, where, c * seg_local:(c + 1) * seg_local, :] = encode(block)
                    else:
                        acc[b, h, where, c * seg_local:(c + 1) * seg_local, :] = block
        if count == n // 2 - 1:
            pl.semaphore_wait(barrier, len(peers) + 1)
            for b in range(AHEAD):
                send_scatter(b, 0, 0)
        if count == 3 * n // 4 - 1:
            for b in range(AHEAD):
                send_scatter(b, 1, 0)

    index = me * width + lax.broadcasted_iota(jnp.int32, (orders_count, width), 1)
    order = lax.broadcasted_iota(jnp.int32, (orders_count, width), 0)
    last = order == orders_count - 1
    select = (index >= order * order) & ((index < (order + 1) * (order + 1)) | last)
    chosen = jnp.where(select, 1.0, 0.0).astype(jnp.float32)
    for t, table in enumerate((mag[...], jnp.cos(phase[...]), jnp.sin(phase[...]))):
        tables[t] = jnp.dot(
            table, chosen, precision=lax.Precision.HIGHEST, preferred_element_type=jnp.float32
        )
    tables[3] = noise[:, pl.ds(pl.multiple_of(me * width, width), width)]
    for r in range(n):
        loads["s", r].wait()

    def reduce_step(b, j):
        half = n >> (j + 1)
        low = half // 2 if j == 0 else 1
        for h in range(2):
            scatter[b, h, j].wait_recv()
            if j == 0 and b + AHEAD < bins:
                send_scatter(b + AHEAD, h, 0)
            code_out[b, h, low:half] = encode(
                acc[b, h, low:half] + decode(code_in[b, h, half + low:2 * half])
            )
            if j == 0:
                send_scatter(b, h, 1)
            else:
                send_rest(b, h, lambda q: code_out.at[b, h, q], code_in, scatter, rs_send, rs_recv)
        for h in range(2):
            acc[b, h, 0:low] = acc[b, h, 0:low] + decode(code_in[b, h, half:half + low])

    def power_step(b):
        for h in range(2):
            coeff = acc[b, h, 0]
            for q in range(1, rest):
                scatter[b, h, 1 + q].wait_recv()
                coeff = coeff + decode(code_in[b, h, q])
            acc[b, h, 0] = coeff
            power_out[b, h] = jnp.sum((coeff * coeff).reshape(rows // 8, 8, HALF), axis=0)
        powers[b] = remote(power_out.at[b], power_in.at[b], pw_send.at[b], pw_recv.at[b], other)

    def equalize_step(b):
        powers[b].wait_recv()
        for h in range(2):
            power = jnp.sum(power_out[b, h] + power_in[b, h], axis=0, keepdims=True) / segments
            lanes = slice(h * HALF, (h + 1) * HALF)
            gain = power / (power + tables[3, b:b + 1, lanes]) / tables[0, b:b + 1, lanes]
            cosine, sine = tables[1, b:b + 1, lanes], tables[2, b:b + 1, lanes]
            real, imag = acc[b, h, 0, 0:seg_local, :], acc[b, h, 0, seg_local:rows, :]
            gathered[b, h, 0, 0:seg_local, :] = (gain * (real * cosine + imag * sine)).astype(jnp.bfloat16)
            gathered[b, h, 0, seg_local:rows, :] = (gain * (imag * cosine - real * sine)).astype(jnp.bfloat16)
            send_rest(b, h, lambda q: gathered.at[b, h, 0], gathered, gather, ag_send, ag_recv)

    def forward_step(b, j):
        for h in range(2):
            for k in ([1] if j == 0 else range(2, 1 + rest)):
                gather[b, h, k].wait_recv()
            send_gather(b, h, j)

    def beam_step(b):
        for h in range(2):
            gather[b, h, 0].wait_recv()
        beam = jnp.zeros((rows, out.shape[1]), jnp.float32)
        for r in range(n):
            left = jnp.concatenate([gathered[b, 0, slot(0, r)], gathered[b, 1, slot(1, r)]], axis=1)
            beam = beam + jnp.dot(left, sbuf[r], preferred_element_type=jnp.float32)
        beam_out[b] = jnp.sum((beam * beam).reshape(rows // 8, 8, out.shape[1]), axis=0)

    steps = (
        None, lambda b: reduce_step(b, 0), lambda b: reduce_step(b, 1), power_step, equalize_step,
        lambda b: forward_step(b, 1), lambda b: forward_step(b, 0), beam_step,
    )
    for b, step in schedule(bins):
        steps[step](b)

    final = remote(beam_out, beam_in, bm_send.at[0], bm_recv.at[0], other)
    final.wait_recv()
    for b in range(bins):
        out[b:b + 1, :] = jnp.sum(beam_out[b] + beam_in[b], axis=0, keepdims=True) / segments
    for copy in sends:
        copy.wait_send()


def fused(n, bits, pressure, harmonics, steering, radial_mag, radial_phase, noise):
    _, bins, seg_local, mics = pressure.shape
    rows = 2 * seg_local
    dirs = steering.shape[1]
    width = 2 * HALF
    f32, bf16 = jnp.float32, jnp.bfloat16
    dma = pltpu.SemaphoreType.DMA
    anywhere, vmem = pl.BlockSpec(memory_space=pltpu.HBM), pl.BlockSpec(memory_space=pltpu.VMEM)
    return pl.pallas_call(
        functools.partial(kernel, n, bits, seg_local),
        out_shape=jax.ShapeDtypeStruct((bins, dirs), f32),
        in_specs=[anywhere] * 3 + [vmem] * 3,
        out_specs=vmem,
        scratch_shapes=[
            pltpu.VMEM((rows * bins, mics), bf16),
            pltpu.VMEM((n, mics, width), bf16),
            pltpu.VMEM((n, width, dirs), bf16),
            pltpu.VMEM((4, bins, width), f32),
            pltpu.VMEM((bins, 2, n // 2, rows, HALF), f32),
            pltpu.VMEM((bins, 2, n, rows, HALF), bf16),
            pltpu.VMEM((bins, 2, n, rows, HALF), bf16),
            pltpu.VMEM((bins, 2, n, rows, HALF), bf16),
            pltpu.VMEM((bins, 2, 8, HALF), f32),
            pltpu.VMEM((bins, 2, 8, HALF), f32),
            pltpu.VMEM((bins, 8, dirs), f32),
            pltpu.VMEM((bins, 8, dirs), f32),
            dma((1 + 2 * n,)),
            dma((bins, 2, 1 + n // 4)),
            dma((bins, 2, 1 + n // 4)),
            dma((bins, 2, 1 + n // 4)),
            dma((bins, 2, 1 + n // 4)),
            dma((bins,)),
            dma((bins,)),
            dma((1,)),
            dma((1,)),
        ],
        compiler_params=pltpu.CompilerParams(
            collective_id=0, has_side_effects=True, vmem_limit_bytes=44 * 2**20
        ),
    )(
        pressure.reshape(rows * bins, mics), harmonics, steering,
        radial_mag, radial_phase, noise,
    )


def solution(mesh):
    placed = (P(None, None, "seg", "mic"), P("mic", None), P(None, "mic"), P(), P(), P())
    n = mesh.shape["mic"]
    bits = n.bit_length() - 1

    def run(pressure, harmonics, *rest):
        fits = n == 1 << bits and bits >= 3 and harmonics.shape[1] == 2 * HALF * n
        fits = fits and mesh.shape["seg"] == 2 and pressure.shape[2] % 16 == 0
        if fits:
            return fused(n, bits, pressure, harmonics, *rest)
        return shards(pressure, harmonics, *rest)

    return jax.shard_map(
        run, mesh=mesh, in_specs=placed, out_specs=P(None, "mic"), check_vma=False
    )
```

```python
import functools

import jax
import jax.numpy as jnp
from jax import lax
from jax.experimental import pallas as pl
from jax.experimental.pallas import tpu as pltpu
from jax.sharding import PartitionSpec as P

MESH = pl.DeviceIdType.MESH
HALF = 128
BINS = 4
STEPS = (
    "0a 1a 0b 01",
    "11 1b 2a 02",
    "3a 12 2b 21",
    "03 04 13 31",
    "14 3b 22 05",
    "06 32 15 23",
    "24 1g 0g 33",
    "16 34 25 2g",
    "35 26 07 3g",
    "36 27 17 37",
)


def order_lookup(table, count, start):
    orders = table.shape[1]
    index = start + jnp.arange(count, dtype=jnp.int32)
    squares = jnp.arange(1, orders, dtype=jnp.int32) ** 2
    level = jnp.sum((index[:, None] >= squares[None, :]).astype(jnp.int32), axis=1)
    select = level[:, None] == jnp.arange(orders, dtype=jnp.int32)[None, :]
    return jnp.sum(jnp.where(select[:, None, :], table[None, :, :], jnp.float32(0.0)), axis=2)


def shards(pressure, harmonics, steering, radial_mag, radial_phase, noise):
    bins = pressure.shape[1]
    seg_local = pressure.shape[2]
    rows = 2 * bins * seg_local
    segments = seg_local * lax.axis_size("seg")
    flat = pressure.reshape(rows, pressure.shape[3])
    local_terms = lax.dot_general(
        harmonics, flat, (((0,), (1,)), ((), ())), preferred_element_type=jnp.float32
    )
    owned = lax.psum_scatter(local_terms, "mic", scatter_dimension=0, tiled=True)
    count = owned.shape[0]
    first = lax.axis_index("mic") * count
    coeff = owned.reshape(count, 2, bins, seg_local)
    local_power = jnp.sum(coeff[:, 0] * coeff[:, 0] + coeff[:, 1] * coeff[:, 1], axis=2)
    power = lax.psum(local_power, "seg") / segments
    noise_part = lax.dynamic_slice_in_dim(noise, first, count, 1).T
    mag = order_lookup(radial_mag, count, first)
    phi = order_lookup(radial_phase, count, first)
    gain = (power / (power + noise_part) / mag)[:, :, None]
    cosine = jnp.cos(phi)[:, :, None]
    sine = jnp.sin(phi)[:, :, None]
    real_part = gain * (coeff[:, 0] * cosine + coeff[:, 1] * sine)
    imag_part = gain * (coeff[:, 1] * cosine - coeff[:, 0] * sine)
    equalized = jnp.stack([real_part, imag_part], axis=1).astype(jnp.bfloat16).reshape(count, rows)
    equalized = lax.all_gather(equalized, "mic", axis=0, tiled=True)
    beam = lax.dot_general(
        steering, equalized, (((0,), (0,)), ((), ())), preferred_element_type=jnp.float32
    )
    beam = beam.reshape(steering.shape[1], 2, bins, seg_local)
    local_beam = jnp.sum(beam[:, 0] * beam[:, 0] + beam[:, 1] * beam[:, 1], axis=2)
    total = lax.psum(local_beam, "seg") / segments
    return total.T


def encode(value):
    square = value * value
    return (square * (value * jnp.abs(value))).astype(jnp.bfloat16)


def decode(code):
    code = code.astype(jnp.float32)
    size = jnp.abs(code)
    root = lax.rsqrt(lax.rsqrt(jnp.maximum(size, 1e-37)))
    return jnp.where(code < 0, -root, jnp.where(code > 0, root, 0.0))


def kernel(
    n, bits, seg_local,
    pressure, harmonics, steering, mag_far, phase_far, noise_far, out,
    pbuf, hbuf, sbuf, mag, phase, noise, tables, acc, code_out, code_in, gathered,
    power_out, power_in, beam_out, beam_in,
    local_sem, rs_send, rs_recv, ag_send, ag_recv, pw_send, pw_recv, bm_send, bm_recv,
):
    bins, orders_count = mag_far.shape
    rows = 2 * seg_local
    segments = seg_local * 2
    me, core = lax.axis_index("mic"), lax.axis_index("seg")
    step_of = [(1 << b) * (1 - 2 * ((me // (1 << b)) % 2)) for b in range(bits)]
    rest = n // 4

    def owner(r):
        return me + sum(step_of[b] for b in range(bits) if (r >> b) & 1)

    def slot(h, r):
        x, y = r & 1, (r >> 1) & 1
        return (r >> 2) + rest * ((2 * x + y) if h == 0 else (2 * y + x))

    def near(r):
        return (owner(r), core)

    other = (me, 1 - core)

    sequence = sorted(range(n), key=lambda r: (-(r & 1), -(r & 2), r))
    width = 2 * HALF
    loads = {"p": pltpu.make_async_copy(pressure, pbuf, local_sem.at[0])}
    loads["p"].start()
    for r in sequence:
        first = pl.multiple_of(owner(r) * width, width)
        loads["h", r] = pltpu.make_async_copy(
            harmonics.at[:, pl.ds(first, width)], hbuf.at[r], local_sem.at[1 + r]
        )
        loads["h", r].start()
    small = []
    first = pl.multiple_of(me * width, width)
    for i, (src, dst) in enumerate(
        ((mag_far, mag), (phase_far, phase), (noise_far.at[:, pl.ds(first, width)], noise))
    ):
        small.append(pltpu.make_async_copy(src, dst, local_sem.at[1 + 2 * n + i]))
        small[-1].start()
    barrier = pltpu.get_barrier_semaphore()
    peers = [1, 2] + [4 * q for q in range(1, rest)]
    for r in peers:
        pl.semaphore_signal(barrier, inc=1, device_id=near(r), device_id_type=MESH)
    pl.semaphore_signal(barrier, inc=1, device_id=other, device_id_type=MESH)
    for r in range(n):
        first = pl.multiple_of(owner(r) * width, width)
        loads["s", r] = pltpu.make_async_copy(
            steering.at[pl.ds(first, width), :], sbuf.at[r], local_sem.at[1 + n + r]
        )
        loads["s", r].start()

    sends = []

    def remote(src, dst, send_sem, recv_sem, device):
        copy = pltpu.make_async_remote_copy(
            src_ref=src, dst_ref=dst, send_sem=send_sem, recv_sem=recv_sem,
            device_id=device, device_id_type=MESH,
        )
        copy.start()
        sends.append(copy)
        return copy

    scatter, gather, powers = {}, {}, {}

    quarter, half = n // 4, n // 2

    def send_scatter(b, h, j, name, first):
        piece = pl.ds(first, quarter)
        scatter[b, h, name] = remote(
            code_out.at[b, h, piece], code_in.at[b, h, piece],
            rs_send.at[b, h, name], rs_recv.at[b, h, name], near(1 + (h ^ j)),
        )

    def send_gather(b, h, j, name, first):
        gather[b, h, name] = remote(
            gathered.at[b, h, pl.ds(first, quarter)],
            gathered.at[b, h, pl.ds(first + (half >> j), quarter)],
            ag_send.at[b, h, name], ag_recv.at[b, h, name], near(1 + (h ^ j)),
        )

    def send_rest(b, h, first, target, group, send_sem, recv_sem):
        for q in range(1, rest):
            group[b, h, 2 + q] = remote(
                first(q), target.at[b, h, q],
                send_sem.at[b, h, 2 + q], recv_sem.at[b, h, 2 + q], near(4 * q),
            )

    events = " ".join(STEPS).split()
    events = [(int(event[0]), event[1]) for event in events]
    early = 0
    while events[early][1] in "ab":
        early += 1

    def first_step(b, h, name):
        send_scatter(b, h, 0, "ab".index(name), half + quarter if name == "a" else half)

    def early_steps(h):
        for b, name in events[:early]:
            first_step(b, h, name)

    loads["p"].wait()
    for count, r in enumerate(sequence):
        loads["h", r].wait()
        part = jnp.dot(pbuf[...], hbuf[r], preferred_element_type=jnp.float32)
        for h in range(2):
            where = slot(h, r)
            for b in range(bins):
                for c in range(2):
                    first = (c * bins + b) * seg_local
                    block = part[first:first + seg_local, h * HALF:(h + 1) * HALF]
                    if where >= n // 2:
                        code_out[b, h, where, c * seg_local:(c + 1) * seg_local, :] = encode(block)
                    else:
                        acc[b, h, where, c * seg_local:(c + 1) * seg_local, :] = block
        if count == n // 2 - 1:
            pl.semaphore_wait(barrier, len(peers) + 1)
            early_steps(0)
        if count == 3 * n // 4 - 1:
            early_steps(1)

    for load in small:
        load.wait()
    index = me * width + lax.broadcasted_iota(jnp.int32, (orders_count, width), 1)
    order = lax.broadcasted_iota(jnp.int32, (orders_count, width), 0)
    last = order == orders_count - 1
    select = (index >= order * order) & ((index < (order + 1) * (order + 1)) | last)
    chosen = jnp.where(select, 1.0, 0.0).astype(jnp.float32)
    for t, table in enumerate((mag[...], jnp.cos(phase[...]), jnp.sin(phase[...]))):
        tables[t] = jnp.dot(
            table, chosen, precision=lax.Precision.HIGHEST, preferred_element_type=jnp.float32
        )
    tables[3] = noise[...]
    for r in range(n):
        loads["s", r].wait()

    def reduce_first(b):
        for h in range(2):
            scatter[b, h, 0].wait_recv()
            code_out[b, h, quarter:half] = encode(
                acc[b, h, quarter:half] + decode(code_in[b, h, half + quarter:n])
            )
            send_scatter(b, h, 1, 2, quarter)

    def reduce_second(b):
        for h in range(2):
            scatter[b, h, 1].wait_recv()
            acc[b, h, 0:quarter] = acc[b, h, 0:quarter] + decode(code_in[b, h, half:half + quarter])
        for h in range(2):
            scatter[b, h, 2].wait_recv()
            code_out[b, h, 1:quarter] = encode(
                acc[b, h, 1:quarter] + decode(code_in[b, h, quarter + 1:half])
            )
            send_rest(b, h, lambda q: code_out.at[b, h, q], code_in, scatter, rs_send, rs_recv)
        for h in range(2):
            acc[b, h, 0] = acc[b, h, 0] + decode(code_in[b, h, quarter])

    def power_step(b):
        for h in range(2):
            coeff = acc[b, h, 0]
            for q in range(1, rest):
                scatter[b, h, 2 + q].wait_recv()
                coeff = coeff + decode(code_in[b, h, q])
            acc[b, h, 0] = coeff
            power_out[b, h] = jnp.sum((coeff * coeff).reshape(rows // 8, 8, HALF), axis=0)
        powers[b] = remote(power_out.at[b], power_in.at[b], pw_send.at[b], pw_recv.at[b], other)

    def equalize_step(b):
        powers[b].wait_recv()
        for h in range(2):
            power = jnp.sum(power_out[b, h] + power_in[b, h], axis=0, keepdims=True) / segments
            lanes = slice(h * HALF, (h + 1) * HALF)
            gain = power / (power + tables[3, b:b + 1, lanes]) / tables[0, b:b + 1, lanes]
            cosine, sine = tables[1, b:b + 1, lanes], tables[2, b:b + 1, lanes]
            real, imag = acc[b, h, 0, 0:seg_local, :], acc[b, h, 0, seg_local:rows, :]
            gathered[b, h, 0, 0:seg_local, :] = (gain * (real * cosine + imag * sine)).astype(jnp.bfloat16)
            gathered[b, h, 0, seg_local:rows, :] = (gain * (imag * cosine - real * sine)).astype(jnp.bfloat16)
            send_rest(b, h, lambda q: gathered.at[b, h, 0], gathered, gather, ag_send, ag_recv)

    def forward_first(b):
        for h in range(2):
            for q in range(1, rest):
                gather[b, h, 2 + q].wait_recv()
            send_gather(b, h, 1, 2, 0)

    def forward_own(b):
        for h in range(2):
            send_gather(b, h, 0, 0, 0)

    def forward_second(b):
        for h in range(2):
            gather[b, h, 2].wait_recv()
            send_gather(b, h, 0, 1, quarter)

    def beam_step(b):
        for h in range(2):
            gather[b, h, 0].wait_recv()
            gather[b, h, 1].wait_recv()
        beam = jnp.zeros((rows, out.shape[1]), jnp.float32)
        for r in range(n):
            left = jnp.concatenate([gathered[b, 0, slot(0, r)], gathered[b, 1, slot(1, r)]], axis=1)
            beam = beam + jnp.dot(left, sbuf[r], preferred_element_type=jnp.float32)
        beam_out[b] = jnp.sum((beam * beam).reshape(rows // 8, 8, out.shape[1]), axis=0)

    steps = {
        "1": reduce_first, "2": reduce_second, "3": power_step, "4": equalize_step,
        "5": forward_first, "g": forward_own, "6": forward_second, "7": beam_step,
    }
    for b, name in events[early:]:
        if name in steps:
            steps[name](b)
        else:
            first_step(b, 0, name)
            first_step(b, 1, name)

    final = remote(beam_out, beam_in, bm_send.at[0], bm_recv.at[0], other)
    final.wait_recv()
    for b in range(bins):
        out[b:b + 1, :] = jnp.sum(beam_out[b] + beam_in[b], axis=0, keepdims=True) / segments
    for copy in sends:
        copy.wait_send()


def fused(n, bits, pressure, harmonics, steering, radial_mag, radial_phase, noise):
    _, bins, seg_local, mics = pressure.shape
    rows = 2 * seg_local
    dirs = steering.shape[1]
    width = 2 * HALF
    f32, bf16 = jnp.float32, jnp.bfloat16
    dma = pltpu.SemaphoreType.DMA
    anywhere, vmem = pl.BlockSpec(memory_space=pltpu.HBM), pl.BlockSpec(memory_space=pltpu.VMEM)
    return pl.pallas_call(
        functools.partial(kernel, n, bits, seg_local),
        out_shape=jax.ShapeDtypeStruct((bins, dirs), f32),
        in_specs=[anywhere] * 6,
        out_specs=vmem,
        scratch_shapes=[
            pltpu.VMEM((rows * bins, mics), bf16),
            pltpu.VMEM((n, mics, width), bf16),
            pltpu.VMEM((n, width, dirs), bf16),
            pltpu.VMEM(radial_mag.shape, f32),
            pltpu.VMEM(radial_mag.shape, f32),
            pltpu.VMEM((bins, width), f32),
            pltpu.VMEM((4, bins, width), f32),
            pltpu.VMEM((bins, 2, n // 2, rows, HALF), f32),
            pltpu.VMEM((bins, 2, n, rows, HALF), bf16),
            pltpu.VMEM((bins, 2, n, rows, HALF), bf16),
            pltpu.VMEM((bins, 2, n, rows, HALF), bf16),
            pltpu.VMEM((bins, 2, 8, HALF), f32),
            pltpu.VMEM((bins, 2, 8, HALF), f32),
            pltpu.VMEM((bins, 8, dirs), f32),
            pltpu.VMEM((bins, 8, dirs), f32),
            dma((4 + 2 * n,)),
            dma((bins, 2, 2 + n // 4)),
            dma((bins, 2, 2 + n // 4)),
            dma((bins, 2, 2 + n // 4)),
            dma((bins, 2, 2 + n // 4)),
            dma((bins,)),
            dma((bins,)),
            dma((1,)),
            dma((1,)),
        ],
        compiler_params=pltpu.CompilerParams(
            collective_id=0, has_side_effects=True, vmem_limit_bytes=63 * 2**20
        ),
    )(
        pressure.reshape(rows * bins, mics), harmonics, steering,
        radial_mag, radial_phase, noise,
    )


def solution(mesh):
    placed = (P(None, None, "seg", "mic"), P("mic", None), P(None, "mic"), P(), P(), P())
    n = mesh.shape["mic"]
    bits = n.bit_length() - 1

    def run(pressure, harmonics, *rest):
        fits = n == 1 << bits and bits >= 3 and pressure.shape[1] == BINS and harmonics.shape[1] == 2 * HALF * n
        fits = fits and mesh.shape["seg"] == 2 and pressure.shape[2] % 16 == 0
        if fits:
            return fused(n, bits, pressure, harmonics, *rest)
        return shards(pressure, harmonics, *rest)

    return jax.shard_map(
        run, mesh=mesh, in_specs=placed, out_specs=P(None, "mic"), check_vma=False
    )
```
